32 devices in a mesh: seq: 16 (over z, y, x), batch: 2 (over core).
Axes of the slice: x: 2, y: 2, z: 4, core: 2. Of those that a mesh axis runs over, the one named last changes fastest.
Arguments:
- inputs: bfloat16 [8, 2048, 512], P('batch', 'seq'), may hold values from -6 to 6
- out_grad: bfloat16 [8, 2048, 512], P('batch', 'seq'), may hold values from -6 to 6
- log_rate: float32 [512, 64], replicated, as said below
- pole_angle: float32 [512, 64], replicated, may hold values from -3.140625 to 3.140625
- weight_real: float32 [512, 64], replicated, may hold values from -0.75 to 0.75
- weight_imag: float32 [512, 64], replicated, may hold values from -0.75 to 0.75
- passthrough: float32 [512], replicated, may hold values from -4 to 4
Outputs:
- input_grad: bfloat16 [8, 2048, 512], P('batch', 'seq')
- rate_grad: float32 [512, 64], replicated
- angle_grad: float32 [512, 64], replicated
- weight_real_grad: float32 [512, 64], replicated
- weight_imag_grad: float32 [512, 64], replicated
- passthrough_grad: float32 [512], replicated
The draws below stay inside these ranges and needn't reach their ends.
Inputs may be any that keep to these rules, and one draw needn't show every extreme that they name: `log_rate`: every entry lies between the natural logarithm of 0.0001 and the natural logarithm of 0.08.
All inputs are finite; a program needn't handle non-finite values.
Results may differ from the reference program's by a relative error of at most 0.0064.
Values may be sent and summed in bfloat16 or wider, within the bound.
A program may use at most 64 MiB of HBM per device.

```python
import math
import jax
import jax.numpy as jnp
from jax import lax

CH = 512
STATE = 64
LC = 128
BATCH = 8
SEQLEN = 2048
NFREQ = 4096
FREQ_ROWS = 32
N_SEQ = 16


def draw_log_rate(key, part):
    key = jax.random.fold_in(key, 7)
    pick_key, slow_key, fast_key = jax.random.split(key, 3)
    slow_share = 0.5
    middle = math.log(max(2.3 / SEQLEN, 0.0003))
    slow = jax.random.uniform(pick_key, (CH, STATE), jnp.float32) < slow_share
    slow_values = jax.random.uniform(slow_key, (CH, STATE), jnp.float32, minval=math.log(0.0001), maxval=middle)
    fast_values = jax.random.uniform(fast_key, (CH, STATE), jnp.float32, minval=middle, maxval=math.log(0.08))
    return jnp.where(slow, slow_values, fast_values).astype(jnp.float32)


def levels(key, extent, cuts, smallest, high):
    def one(dim, shards_of):
        steps = jax.random.uniform(jax.random.fold_in(jax.random.fold_in(key, 6), dim), (shards_of,), jnp.float32, smallest / len(cuts), high / len(cuts))
        return jnp.repeat(jnp.exp(steps), extent[dim] // shards_of).reshape((-1,) + (1,) * (len(extent) - dim - 1))

    gain = one(*cuts[0])
    for cut in cuts[1:]:
        gain = gain * one(*cut)
    return gain


def gaussian(stream_key, extent, spread, bound, cuts=(), held_as=jnp.bfloat16):
    level = levels(stream_key, extent, cuts, -0.22, 0.18) if cuts else 1.0
    values = jax.random.normal(stream_key, extent, jnp.float32) * spread * level
    return jnp.minimum(jnp.maximum(values, -bound), bound).astype(held_as)


def setup_inputs(seed: int = 0) -> dict:
    keys = jax.random.split(jax.random.key(seed), 8)
    return {
        "inputs": gaussian(keys[0], (BATCH, SEQLEN, CH), 1.0, 6.0, ((0, 2), (1, 16))),
        "out_grad": gaussian(keys[1], (BATCH, SEQLEN, CH), 1.0, 6.0, ((0, 2), (1, 16))),
        "log_rate": draw_log_rate(jax.random.fold_in(keys[7], 71), 0),
        "pole_angle": jnp.clip(jax.random.uniform(keys[3], (CH, STATE), jnp.float32, -3.140625, 3.140625), -3.140625, 3.140625),
        "weight_real": gaussian(keys[4], (CH, STATE), 0.125, 0.75, (), jnp.float32),
        "weight_imag": gaussian(keys[5], (CH, STATE), 0.125, 0.75, (), jnp.float32),
        "passthrough": gaussian(keys[6], (CH,), 1.0, 4.0, (), jnp.float32),
    }


TWO_PI = 2.0 * math.pi
block_len = 512

def cos_sin(numerator, length):
    phases = (numerator % length).astype(jnp.float32) * (TWO_PI / length)
    return (jnp.cos(phases), -jnp.sin(phases))

def rounded(values):
    return lax.optimization_barrier(values.astype(jnp.bfloat16)).astype(jnp.float32)

def spectrum_terms(parameters, z_real, z_imag):
    log_rate, pole_angle, weight_real, weight_imag = parameters
    log_rate = log_rate.T
    pole_angle = pole_angle.T
    weight_real = weight_real.T
    weight_imag = weight_imag.T
    rate = jnp.exp(log_rate)
    radius = jnp.exp(-rate)
    pole_real = radius * jnp.cos(pole_angle)
    pole_imag = radius * jnp.sin(pole_angle)
    shrink = jnp.sqrt(-jnp.expm1(-2.0 * rate))
    scaled_real = weight_real * shrink
    scaled_imag = weight_imag * shrink
    z_real = z_real[:, None, None]
    z_imag = z_imag[:, None, None]
    diff_real = z_real - pole_real
    diff_upper = z_imag - pole_imag
    diff_lower = z_imag + pole_imag
    inv_upper = 1.0 / (diff_real * diff_real + diff_upper * diff_upper)
    inv_lower = 1.0 / (diff_real * diff_real + diff_lower * diff_lower)
    part_real = (scaled_real * diff_real + scaled_imag * diff_upper) * inv_upper + (scaled_real * diff_real - scaled_imag * diff_lower) * inv_lower
    part_imag = (scaled_imag * diff_real - scaled_real * diff_upper) * inv_upper - (scaled_imag * diff_real + scaled_real * diff_lower) * inv_lower
    return (lax.optimization_barrier(jnp.sum(part_real, axis=1)), lax.optimization_barrier(jnp.sum(part_imag, axis=1)))

def kernel_block(parameters, offset):
    frequency = offset + jnp.arange(block_len, dtype=jnp.int32)
    phases = frequency.astype(jnp.float32) * (TWO_PI / NFREQ)
    return spectrum_terms(parameters, jnp.cos(phases), jnp.sin(phases))

def contract(form, left, right):
    return jnp.einsum(form, left, right, precision=lax.Precision.HIGHEST)

def reference(inputs, out_grad, log_rate, pole_angle, weight_real, weight_imag, passthrough):
    parameters = (log_rate, pole_angle, weight_real, weight_imag)
    row_index = jnp.arange(N_SEQ, dtype=jnp.int32)
    col_index = jnp.arange(FREQ_ROWS, dtype=jnp.int32)
    positions = jnp.arange(LC, dtype=jnp.int32)
    cos_one, sin_one = cos_sin(row_index[:, None] * col_index[None, :], FREQ_ROWS)
    cos_one = rounded(cos_one)
    sin_one = rounded(sin_one)
    cos_two, sin_two = cos_sin(positions[:, None] * positions[None, :], LC)
    cos_two = rounded(cos_two)
    sin_two = rounded(sin_two)
    turn_real, turn_imag = cos_sin(positions[:, None] * col_index[None, :], NFREQ)
    turn_real = turn_real[:, :, None]
    turn_imag = turn_imag[:, :, None]
    starts = jnp.arange(NFREQ // block_len, dtype=jnp.int32) * block_len
    kern_real, kern_imag = lax.map(lambda offset: kernel_block(parameters, offset), starts)
    kern_real = kern_real.reshape(LC, FREQ_ROWS, CH)
    kern_imag = kern_imag.reshape(LC, FREQ_ROWS, CH)

    def forward(signal):
        blocks = signal.reshape(N_SEQ, LC, CH).astype(jnp.float32)
        part_real = contract('rmc,rk->mkc', blocks, cos_one)
        part_imag = contract('rmc,rk->mkc', blocks, sin_one)
        g_real = rounded(part_real * turn_real - part_imag * turn_imag)
        g_imag = rounded(part_real * turn_imag + part_imag * turn_real)
        spec_real = contract('mkc,mq->qkc', g_real, cos_two) - contract('mkc,mq->qkc', g_imag, sin_two)
        spec_imag = contract('mkc,mq->qkc', g_real, sin_two) + contract('mkc,mq->qkc', g_imag, cos_two)
        return (spec_real, spec_imag)

    def one_sample(running, sample):
        signal, cotangent = sample
        in_real, in_imag = forward(signal)
        out_real, out_imag = forward(cotangent)
        grad_real = running[0] + (out_real * in_real + out_imag * in_imag)
        grad_imag = running[1] + (out_real * in_imag - out_imag * in_real)
        prod_real = rounded((kern_real * out_real + kern_imag * out_imag) / NFREQ)
        prod_imag = rounded((kern_real * out_imag - kern_imag * out_real) / NFREQ)
        back_real = contract('qkc,qm->mkc', prod_real, cos_two) + contract('qkc,qm->mkc', prod_imag, sin_two)
        back_imag = contract('qkc,qm->mkc', prod_imag, cos_two) - contract('qkc,qm->mkc', prod_real, sin_two)
        turned_real = rounded(back_real * turn_real + back_imag * turn_imag)
        turned_imag = rounded(back_imag * turn_real - back_real * turn_imag)
        conv = contract('mkc,rk->rmc', turned_real, cos_one) + contract('mkc,rk->rmc', turned_imag, sin_one)
        conv = rounded(conv).reshape(SEQLEN, CH)
        result = (conv + passthrough * cotangent.astype(jnp.float32)).astype(jnp.bfloat16)
        return ((grad_real, grad_imag), result)
    zeros = jnp.zeros((LC, FREQ_ROWS, CH), jnp.float32)
    sums, input_grad = lax.scan(one_sample, (zeros, zeros), (inputs, out_grad))
    spec_real = (sums[0] / NFREQ).reshape(NFREQ, CH)
    spec_imag = (sums[1] / NFREQ).reshape(NFREQ, CH)

    def grad_step(running, offset):
        slab_real = lax.dynamic_slice_in_dim(spec_real, offset, block_len, 0)
        slab_imag = lax.dynamic_slice_in_dim(spec_imag, offset, block_len, 0)
        unused, pull = jax.vjp(lambda values: kernel_block(values, offset), parameters)
        pulled = pull((slab_real, -slab_imag))[0]
        return (tuple((left + right for left, right in zip(running, pulled))), None)
    initial = tuple((jnp.zeros_like(values) for values in parameters))
    pulled, unused = lax.scan(grad_step, initial, starts)
    passthrough_grad = lax.optimization_barrier(jnp.sum(inputs.astype(jnp.float32) * out_grad.astype(jnp.float32), axis=(0, 1)))
    return (input_grad, pulled[0], pulled[1], pulled[2], pulled[3], passthrough_grad)
```

```python
import math

import jax
import jax.numpy as jnp
from jax import lax
from jax.sharding import PartitionSpec as P

TWO_PI = 2.0 * math.pi
AXES = ("seq", "batch")
HIGH = lax.Precision.HIGH


def cos_sin(numerator, length):
    phases = (numerator % length).astype(jnp.float32) * (TWO_PI / length)
    return (jnp.cos(phases), jnp.sin(phases))


def cmul(a, b):
    return (a[0] * b[0] - a[1] * b[1], a[0] * b[1] + a[1] * b[0])


def cdiv(a, b):
    inv = 1.0 / (b[0] * b[0] + b[1] * b[1])
    return ((a[0] * b[0] + a[1] * b[1]) * inv, (a[1] * b[0] - a[0] * b[1]) * inv)


def powers(rate, angle, step, count):
    turn = angle * step
    laps = jnp.round(turn * (1.0 / TWO_PI))
    turn = (turn - laps * 6.28125) - laps * (TWO_PI - 6.28125)
    n = jnp.arange(count, dtype=jnp.float32)
    size = jnp.exp(-(rate * step)[..., None] * n)
    phase = turn[..., None] * n
    return (size * jnp.cos(phase), size * jnp.sin(phase))


def local(inputs, out_grad, log_rate, pole_angle, weight_real, weight_imag, passthrough):
    batch_rows, slice_len, channels = inputs.shape
    rows = lax.axis_size("seq")
    copies = lax.axis_size("batch")
    devices = rows * copies
    own_ch = channels // devices
    batch = batch_rows * copies
    freq_rows = 2 * rows
    half = rows + 1
    n_freq = freq_rows * slice_len
    me = lax.axis_index("seq") * copies + lax.axis_index("batch")

    def to_channels(x):
        x = x.reshape(batch_rows, slice_len, devices, own_ch).transpose(2, 0, 3, 1)
        x = lax.all_to_all(x, AXES, split_axis=0, concat_axis=0, tiled=True)
        return x.reshape(rows, batch, own_ch, slice_len)

    grad_cols = to_channels(out_grad)
    in_cols = to_channels(inputs)

    k_index = jnp.arange(half, dtype=jnp.int32)
    r_index = jnp.arange(freq_rows, dtype=jnp.int32)
    m_index = jnp.arange(slice_len, dtype=jnp.int32)
    cos_one, sin_one = cos_sin(k_index[:, None] * r_index[None, :], freq_rows)
    table_one = jnp.stack([cos_one, -sin_one], axis=1)
    cos_two, sin_two = cos_sin(m_index[:, None] * m_index[None, :], slice_len)
    turn_real, turn_imag = cos_sin(k_index[:, None] * m_index[None, :], n_freq)
    full_cos = turn_real[:, :, None] * cos_two - turn_imag[:, :, None] * sin_two
    full_sin = turn_imag[:, :, None] * cos_two + turn_real[:, :, None] * sin_two
    table_two = jnp.concatenate(
        [
            jnp.concatenate([full_cos, -full_sin], axis=2),
            jnp.concatenate([full_sin, full_cos], axis=2),
        ],
        axis=1,
    )
    ends = (k_index == 0) | (k_index == rows)
    share = jnp.where(ends, 1.0, 2.0).astype(jnp.float32)[:, None, None] / n_freq
    table_back = table_one * share
    one16 = table_one.astype(jnp.bfloat16)
    two16 = table_two.astype(jnp.bfloat16)
    back16 = (table_one * (share * n_freq)).astype(jnp.bfloat16)

    def own(p):
        return lax.dynamic_slice_in_dim(p, me * own_ch, own_ch, 0)

    rate = jnp.exp(own(log_rate))
    angle = own(pole_angle)
    w_real, w_imag = own(weight_real), own(weight_imag)
    shrink = jnp.sqrt(-jnp.expm1(-2.0 * rate))
    weight = (w_real * shrink, w_imag * shrink)
    fine = powers(rate, angle, 1.0, slice_len)
    coarse = powers(rate, angle, float(slice_len), freq_rows + 1)
    whole = (coarse[0][..., -1], coarse[1][..., -1])
    coarse = (coarse[0][..., :-1], coarse[1][..., :-1])
    lam = (fine[0][..., 1], fine[1][..., 1])
    gap = (1.0 - whole[0], -whole[1])
    bottom = cmul(lam, gap)
    lead = cdiv(weight, bottom)
    tail = 2.0 * jnp.sum(cdiv(weight, lam)[0], axis=1)
    lead_rows = cmul((lead[0][..., None], lead[1][..., None]), coarse)
    taps = jnp.einsum(
        "xsr,xsm->rxm",
        jnp.concatenate([2.0 * lead_rows[0], -2.0 * lead_rows[1]], axis=1),
        jnp.concatenate(fine, axis=1),
        precision=HIGH,
    )
    kern = jnp.einsum("kir,rxm->kxim", table_one, taps, precision=HIGH)
    kern = jnp.einsum("kxa,kab->kxb", kern.reshape(half, own_ch, -1), table_two, precision=HIGH)
    kern_real = kern[:, :, :slice_len] - tail[None, :, None]
    kern_imag = kern[:, :, slice_len:]

    def forward(x):
        g = jnp.einsum("kir,rbxm->kbxim", one16[:, :, :rows], x, preferred_element_type=jnp.float32)
        g = g.astype(jnp.bfloat16).reshape(half, batch, own_ch, 2 * slice_len)
        s = jnp.einsum("kbxa,kac->kbxc", g, two16, preferred_element_type=jnp.float32)
        return s[..., :slice_len], s[..., slice_len:]

    out_real, out_imag = forward(grad_cols)
    kr, ki = kern_real[:, None], kern_imag[:, None]
    prod = jnp.concatenate(
        [(kr * out_real + ki * out_imag) / n_freq, (kr * out_imag - ki * out_real) / n_freq],
        axis=3,
    ).astype(jnp.bfloat16)
    back = jnp.einsum("kbxc,kac->kbxa", prod, two16, preferred_element_type=jnp.float32)
    back = back.astype(jnp.bfloat16).reshape(half, batch, own_ch, 2, slice_len)
    conv = jnp.einsum("kir,kbxim->rbxm", back16[:, :, :rows], back, preferred_element_type=jnp.float32)
    conv = conv.astype(jnp.bfloat16).reshape(devices, batch_rows, own_ch, slice_len)
    conv = lax.all_to_all(conv, AXES, split_axis=0, concat_axis=0, tiled=True)
    conv = conv.transpose(1, 3, 0, 2).reshape(batch_rows, slice_len, channels)
    input_grad = (conv.astype(jnp.float32) + passthrough * out_grad.astype(jnp.float32)).astype(
        jnp.bfloat16
    )

    in_real, in_imag = forward(in_cols)
    cross = jnp.concatenate(
        [
            jnp.sum(out_real * in_real + out_imag * in_imag, axis=1),
            jnp.sum(out_imag * in_real - out_real * in_imag, axis=1),
        ],
        axis=2,
    )
    corr = jnp.einsum("kxc,kac->kxa", cross, table_two, precision=HIGH)
    corr = jnp.einsum(
        "kir,kxim->xrm", table_back, corr.reshape(half, own_ch, 2, slice_len), precision=HIGH
    )
    steps = jnp.arange(slice_len, dtype=jnp.float32)
    sums = jnp.einsum(
        "xsm,xrm->xsr",
        jnp.concatenate([fine[0], fine[1], steps * fine[0], steps * fine[1]], axis=1),
        corr,
        precision=HIGH,
    )
    states = rate.shape[1]
    low = (sums[:, :states], sums[:, states : 2 * states])
    low_step = (sums[:, 2 * states : 3 * states], sums[:, 3 * states :])
    far = jnp.arange(freq_rows, dtype=jnp.float32) * slice_len
    t0 = tuple(jnp.sum(v, axis=2) for v in cmul(coarse, low))
    t1 = tuple(
        jnp.sum(v, axis=2)
        for v in cmul(coarse, (low[0] * far + low_step[0], low[1] * far + low_step[1]))
    )
    corr0 = corr[:, 0, 0][:, None]
    near = cdiv((corr0, jnp.zeros_like(corr0)), lam)
    top = cdiv(t0, bottom)
    h = (top[0] - near[0], top[1] - near[1])
    d = cdiv(t1, bottom)
    ratio = cdiv((1.0 - (n_freq + 1.0) * whole[0], -(n_freq + 1.0) * whole[1]), gap)
    lower = cmul(top, ratio)
    d = (d[0] - lower[0] + near[0], d[1] - lower[1] + near[1])
    wd = cmul(weight, d)
    wr_grad = 2.0 * shrink * h[0]
    wi_grad = -2.0 * shrink * h[1]
    angle_grad = -2.0 * wd[1]
    shrink_part = 2.0 * (w_real * h[0] - w_imag * h[1]) * jnp.exp(-2.0 * rate) / shrink
    rate_grad = rate * (shrink_part - 2.0 * wd[0])
    pass_part = jnp.sum(
        in_cols.astype(jnp.float32) * grad_cols.astype(jnp.float32), axis=(0, 1, 3)
    )
    packed = jnp.concatenate([rate_grad, angle_grad, wr_grad, wi_grad, jnp.broadcast_to(pass_part[:, None], rate.shape)], axis=1)
    packed = lax.all_gather(packed, AXES, axis=0, tiled=True)
    return (
        input_grad,
        packed[:, :states],
        packed[:, states : 2 * states],
        packed[:, 2 * states : 3 * states],
        packed[:, 3 * states : 4 * states],
        packed[:, 4 * states],
    )


def solution(mesh):
    placed = (P("batch", "seq", None), P("batch", "seq", None), P(), P(), P(), P(), P())
    return jax.shard_map(
        local,
        mesh=mesh,
        in_specs=placed,
        out_specs=(P("batch", "seq", None), P(), P(), P(), P(), P()),
        check_vma=False,
    )
```

```python
import math

import jax
import jax.numpy as jnp
from jax import lax
from jax.experimental import pallas as pl
from jax.experimental.pallas import tpu as pltpu
from jax.sharding import PartitionSpec as P

TWO_PI = 2.0 * math.pi
AXES = ("seq", "batch")
HIGH = lax.Precision.HIGH


def cos_sin(numerator, length):
    phases = (numerator % length).astype(jnp.float32) * (TWO_PI / length)
    return (jnp.cos(phases), jnp.sin(phases))


def cmul(a, b):
    return (a[0] * b[0] - a[1] * b[1], a[0] * b[1] + a[1] * b[0])


def cdiv(a, b):
    inv = 1.0 / (b[0] * b[0] + b[1] * b[1])
    return ((a[0] * b[0] + a[1] * b[1]) * inv, (a[1] * b[0] - a[0] * b[1]) * inv)


def powers(rate, angle, step, count):
    turn = angle * step
    laps = jnp.round(turn * (1.0 / TWO_PI))
    turn = (turn - laps * 6.28125) - laps * (TWO_PI - 6.28125)
    n = jnp.arange(count, dtype=jnp.float32)
    size = jnp.exp(-(rate * step)[..., None] * n)
    phase = turn[..., None] * n
    return (size * jnp.cos(phase), size * jnp.sin(phase))


def peer_of(place, copies):
    return {"seq": place // copies, "batch": place % copies}


def exchange_kernel(devices, copies, conv, grads, conv_out, grads_out, sems):
    me = lax.axis_index("seq") * copies + lax.axis_index("batch")
    barrier = pltpu.get_barrier_semaphore()

    def greet(d, carry):
        pl.semaphore_signal(
            barrier,
            inc=1,
            device_id=peer_of((me + d) % devices, copies),
            device_id_type=pl.DeviceIdType.MESH,
        )
        return carry

    lax.fori_loop(1, devices, greet, 0)
    pl.semaphore_wait(barrier, devices - 1)

    def send(d, carry):
        to = (me + d) % devices
        pltpu.make_async_remote_copy(
            src_ref=grads,
            dst_ref=grads_out.at[me],
            send_sem=sems.at[0],
            recv_sem=sems.at[1],
            device_id=peer_of(to, copies),
            device_id_type=pl.DeviceIdType.MESH,
        ).start()
        pltpu.make_async_remote_copy(
            src_ref=conv.at[to],
            dst_ref=conv_out.at[me],
            send_sem=sems.at[2],
            recv_sem=sems.at[3],
            device_id=peer_of(to, copies),
            device_id_type=pl.DeviceIdType.MESH,
        ).start()
        return carry

    lax.fori_loop(1, devices, send, 0)
    keep = pltpu.make_async_copy(conv.at[me], conv_out.at[me], sems.at[4])
    keep.start()
    grads_out[me] = grads[...]
    keep.wait()
    others = pl.ds(0, devices - 1)
    for sem in (0, 1):
        pltpu.make_async_copy(grads_out.at[others], grads_out.at[others], sems.at[sem]).wait()
    for sem in (2, 3):
        pltpu.make_async_copy(conv_out.at[others], conv_out.at[others], sems.at[sem]).wait()


def exchange(devices, copies, conv, grads):
    return pl.pallas_call(
        lambda *refs: exchange_kernel(devices, copies, *refs),
        out_shape=(
            jax.ShapeDtypeStruct(conv.shape, conv.dtype),
            jax.ShapeDtypeStruct((devices,) + grads.shape, grads.dtype),
        ),
        in_specs=[pl.BlockSpec(memory_space=pltpu.VMEM)] * 2,
        out_specs=[pl.BlockSpec(memory_space=pltpu.VMEM)] * 2,
        scratch_shapes=[pltpu.SemaphoreType.DMA((5,))],
        compiler_params=pltpu.CompilerParams(
            collective_id=0, has_side_effects=True, vmem_limit_bytes=48 * 1024 * 1024
        ),
        name="exchange",
    )(conv, grads)


def local(inputs, out_grad, log_rate, pole_angle, weight_real, weight_imag, passthrough):
    batch_rows, slice_len, channels = inputs.shape
    rows = lax.axis_size("seq")
    copies = lax.axis_size("batch")
    devices = rows * copies
    own_ch = channels // devices
    batch = batch_rows * copies
    freq_rows = 2 * rows
    half = rows + 1
    n_freq = freq_rows * slice_len
    me = lax.axis_index("seq") * copies + lax.axis_index("batch")

    def to_parts(x):
        x = x.reshape(batch_rows, slice_len, devices, own_ch)
        return x.transpose(2, 0, 3, 1).reshape(devices, 1, batch_rows * own_ch, slice_len)

    both = jnp.concatenate([to_parts(out_grad), to_parts(inputs)], axis=1)
    both = lax.all_to_all(both, AXES, split_axis=0, concat_axis=0, tiled=True)
    grad_cols = both[:, 0].reshape(rows, batch, own_ch, slice_len)
    in_cols = both[:, 1].reshape(rows, batch, own_ch, slice_len)

    k_index = jnp.arange(half, dtype=jnp.int32)
    r_index = jnp.arange(freq_rows, dtype=jnp.int32)
    m_index = jnp.arange(slice_len, dtype=jnp.int32)
    cos_one, sin_one = cos_sin(k_index[:, None] * r_index[None, :], freq_rows)
    table_one = jnp.stack([cos_one, -sin_one], axis=1)
    cos_two, sin_two = cos_sin(m_index[:, None] * m_index[None, :], slice_len)
    turn_real, turn_imag = cos_sin(k_index[:, None] * m_index[None, :], n_freq)
    full_cos = turn_real[:, :, None] * cos_two - turn_imag[:, :, None] * sin_two
    full_sin = turn_imag[:, :, None] * cos_two + turn_real[:, :, None] * sin_two
    table_two = jnp.concatenate(
        [
            jnp.concatenate([full_cos, -full_sin], axis=2),
            jnp.concatenate([full_sin, full_cos], axis=2),
        ],
        axis=1,
    )
    ends = (k_index == 0) | (k_index == rows)
    share = jnp.where(ends, 1.0, 2.0).astype(jnp.float32)[:, None, None] / n_freq
    table_back = table_one * share
    one16 = table_one.astype(jnp.bfloat16)
    two16 = table_two.astype(jnp.bfloat16)
    back16 = (table_one * (share * n_freq)).astype(jnp.bfloat16)

    def own(p):
        return lax.dynamic_slice_in_dim(p, me * own_ch, own_ch, 0)

    rate = jnp.exp(own(log_rate))
    angle = own(pole_angle)
    w_real, w_imag = own(weight_real), own(weight_imag)
    shrink = jnp.sqrt(-jnp.expm1(-2.0 * rate))
    weight = (w_real * shrink, w_imag * shrink)
    fine = powers(rate, angle, 1.0, slice_len)
    coarse = powers(rate, angle, float(slice_len), freq_rows + 1)
    whole = (coarse[0][..., -1], coarse[1][..., -1])
    coarse = (coarse[0][..., :-1], coarse[1][..., :-1])
    lam = (fine[0][..., 1], fine[1][..., 1])
    gap = (1.0 - whole[0], -whole[1])
    bottom = cmul(lam, gap)
    lead = cdiv(weight, bottom)
    tail = 2.0 * jnp.sum(cdiv(weight, lam)[0], axis=1)
    lead_rows = cmul((lead[0][..., None], lead[1][..., None]), coarse)
    taps = jnp.einsum(
        "xsr,xsm->rxm",
        jnp.concatenate([2.0 * lead_rows[0], -2.0 * lead_rows[1]], axis=1),
        jnp.concatenate(fine, axis=1),
        precision=HIGH,
    )
    kern = jnp.einsum("kir,rxm->kxim", table_one, taps, precision=HIGH)
    kern = jnp.einsum("kxa,kab->kxb", kern.reshape(half, own_ch, -1), table_two, precision=HIGH)
    kern_real = kern[:, :, :slice_len] - tail[None, :, None]
    kern_imag = kern[:, :, slice_len:]

    def forward(x):
        g = jnp.einsum("kir,rbxm->kbxim", one16[:, :, :rows], x, preferred_element_type=jnp.float32)
        g = g.astype(jnp.bfloat16).reshape(half, batch, own_ch, 2 * slice_len)
        s = jnp.einsum("kbxa,kac->kbxc", g, two16, preferred_element_type=jnp.float32)
        return s[..., :slice_len], s[..., slice_len:]

    out_real, out_imag = forward(grad_cols)
    kr, ki = kern_real[:, None], kern_imag[:, None]
    prod = jnp.concatenate(
        [(kr * out_real + ki * out_imag) / n_freq, (kr * out_imag - ki * out_real) / n_freq],
        axis=3,
    ).astype(jnp.bfloat16)
    back = jnp.einsum("kbxc,kac->kbxa", prod, two16, preferred_element_type=jnp.float32)
    back = back.astype(jnp.bfloat16).reshape(half, batch, own_ch, 2, slice_len)
    conv = jnp.einsum("kir,kbxim->rbxm", back16[:, :, :rows], back, preferred_element_type=jnp.float32)
    conv = conv.astype(jnp.bfloat16).reshape(devices, batch_rows * own_ch, slice_len)

    in_real, in_imag = forward(in_cols)
    cross = jnp.concatenate(
        [
            jnp.sum(out_real * in_real + out_imag * in_imag, axis=1),
            jnp.sum(out_imag * in_real - out_real * in_imag, axis=1),
        ],
        axis=2,
    )
    corr = jnp.einsum("kxc,kac->kxa", cross, table_two, precision=HIGH)
    corr = jnp.einsum(
        "kir,kxim->xrm", table_back, corr.reshape(half, own_ch, 2, slice_len), precision=HIGH
    )
    steps = jnp.arange(slice_len, dtype=jnp.float32)
    sums = jnp.einsum(
        "xsm,xrm->xsr",
        jnp.concatenate([fine[0], fine[1], steps * fine[0], steps * fine[1]], axis=1),
        corr,
        precision=HIGH,
    )
    states = rate.shape[1]
    low = (sums[:, :states], sums[:, states : 2 * states])
    low_step = (sums[:, 2 * states : 3 * states], sums[:, 3 * states :])
    far = jnp.arange(freq_rows, dtype=jnp.float32) * slice_len
    t0 = tuple(jnp.sum(v, axis=2) for v in cmul(coarse, low))
    t1 = tuple(
        jnp.sum(v, axis=2)
        for v in cmul(coarse, (low[0] * far + low_step[0], low[1] * far + low_step[1]))
    )
    corr0 = corr[:, 0, 0][:, None]
    near = cdiv((corr0, jnp.zeros_like(corr0)), lam)
    top = cdiv(t0, bottom)
    h = (top[0] - near[0], top[1] - near[1])
    d = cdiv(t1, bottom)
    ratio = cdiv((1.0 - (n_freq + 1.0) * whole[0], -(n_freq + 1.0) * whole[1]), gap)
    lower = cmul(top, ratio)
    d = (d[0] - lower[0] + near[0], d[1] - lower[1] + near[1])
    wd = cmul(weight, d)
    wr_grad = 2.0 * shrink * h[0]
    wi_grad = -2.0 * shrink * h[1]
    angle_grad = -2.0 * wd[1]
    shrink_part = 2.0 * (w_real * h[0] - w_imag * h[1]) * jnp.exp(-2.0 * rate) / shrink
    rate_grad = rate * (shrink_part - 2.0 * wd[0])
    pass_part = jnp.sum(
        in_cols.astype(jnp.float32) * grad_cols.astype(jnp.float32), axis=(0, 1, 3)
    )
    pass_cols = jnp.broadcast_to(pass_part[:, None], rate.shape)
    packed = jnp.concatenate(
        [rate_grad, angle_grad, wr_grad, wi_grad, pass_cols, pass_cols], axis=1
    )
    conv, packed = exchange(devices, copies, conv, packed)
    packed = packed.reshape(channels, -1)
    conv = conv.reshape(devices, batch_rows, own_ch, slice_len)
    conv = conv.transpose(1, 3, 0, 2).reshape(batch_rows, slice_len, channels)
    input_grad = (conv.astype(jnp.float32) + passthrough * out_grad.astype(jnp.float32)).astype(
        jnp.bfloat16
    )
    return (
        input_grad,
        packed[:, :states],
        packed[:, states : 2 * states],
        packed[:, 2 * states : 3 * states],
        packed[:, 3 * states : 4 * states],
        packed[:, 4 * states],
    )


def solution(mesh):
    placed = (P("batch", "seq", None), P("batch", "seq", None), P(), P(), P(), P(), P())
    return jax.shard_map(
        local,
        mesh=mesh,
        in_specs=placed,
        out_specs=(P("batch", "seq", None), P(), P(), P(), P(), P()),
        check_vma=False,
    )
```

```python
import math

import jax
import jax.numpy as jnp
from jax import lax
from jax.experimental import pallas as pl
from jax.experimental.pallas import tpu as pltpu
from jax.sharding import PartitionSpec as P

TWO_PI = 2.0 * math.pi
AXES = ("seq", "batch")
HIGH = lax.Precision.HIGH


def cos_sin(numerator, length):
    phases = (numerator % length).astype(jnp.float32) * (TWO_PI / length)
    return (jnp.cos(phases), jnp.sin(phases))


def cmul(a, b):
    return (a[0] * b[0] - a[1] * b[1], a[0] * b[1] + a[1] * b[0])


def cdiv(a, b):
    inv = 1.0 / (b[0] * b[0] + b[1] * b[1])
    return ((a[0] * b[0] + a[1] * b[1]) * inv, (a[1] * b[0] - a[0] * b[1]) * inv)


def powers(rate, angle, step, counts):
    turn = angle * step
    laps = jnp.round(turn * (1.0 / TWO_PI))
    turn = (turn - laps * 6.28125) - laps * (TWO_PI - 6.28125)
    n = counts.astype(jnp.float32)
    size = jnp.exp(-(rate * step)[..., None] * n)
    phase = turn[..., None] * n
    return (size * jnp.cos(phase), size * jnp.sin(phase))


def peer_of(place, copies):
    return {"seq": place // copies, "batch": place % copies}


def nt_dot(left, right):
    return lax.dot_general(
        left, right, (((1,), (1,)), ((), ())), preferred_element_type=jnp.float32
    )


def split_dot(values, table):
    high = values.astype(jnp.bfloat16).astype(jnp.float32)
    low = values - high
    count = values.shape[0]
    if count % 8 == 0:
        both = jnp.concatenate([high, low], axis=0).astype(jnp.bfloat16)
        both = nt_dot(both, table)
        return both[:count] + both[count:]
    return nt_dot(high.astype(jnp.bfloat16), table) + nt_dot(low.astype(jnp.bfloat16), table)


def middle_kernel(
    copies, own_ch, one, back_one, corr_one, x, kern, two, fine, coarse,
    conv_out, sums_out, wide, spec, back, conv, corr_part, corr, passed, pay, sems,
):
    devices, _, part, width = x.shape
    rows = devices // copies
    half = rows + 1
    freq_rows = 2 * rows
    cols = copies * part
    me = lax.axis_index("seq") * copies + lax.axis_index("batch")
    barrier = pltpu.get_barrier_semaphore()

    def greet(d, carry):
        pl.semaphore_signal(
            barrier,
            inc=1,
            device_id=peer_of((me + d) % devices, copies),
            device_id_type=pl.DeviceIdType.MESH,
        )
        return carry

    lax.fori_loop(1, devices, greet, 0)

    def over_batch(values):
        if own_ch % 8 == 0:
            return jnp.sum(values.reshape(cols // own_ch, own_ch, -1), axis=0)
        pick = lax.broadcasted_iota(jnp.int32, (own_ch, cols), 1) % own_ch
        pick = pick == lax.broadcasted_iota(jnp.int32, (own_ch, cols), 0)
        return jnp.dot(
            pick.astype(jnp.float32), values, precision=lax.Precision.HIGHEST,
            preferred_element_type=jnp.float32,
        )

    def widen(signal):
        def one_row(r, carry):
            for c in range(copies):
                wide[r, c * part : (c + 1) * part] = x[r * copies + c, signal].astype(jnp.float32)
            return carry

        lax.fori_loop(0, rows, one_row, 0)

    def spectrum(k):
        def add(r, sums):
            value = wide[r]
            return (sums[0] + one[2 * k, r] * value, sums[1] + one[2 * k + 1, r] * value)

        zero = jnp.zeros((cols, width), jnp.float32)
        g = lax.fori_loop(0, rows, add, (zero, zero), unroll=min(rows, 16))
        g = jnp.concatenate(g, axis=1).astype(jnp.bfloat16)
        return jnp.dot(g, two[k], preferred_element_type=jnp.float32)

    widen(0)

    def out_step(k, carry):
        s = spectrum(k)
        spec[k] = s
        kk = kern[k]
        if own_ch % 8 == 0:
            kk = jnp.broadcast_to(kk[None], (cols // own_ch,) + kk.shape).reshape(cols, 2 * width)
        sr, si, kr, ki = s[:, :width], s[:, width:], kk[:, :width], kk[:, width:]
        prod = jnp.concatenate([kr * sr + ki * si, kr * si - ki * sr], axis=1)
        back[k] = nt_dot(prod.astype(jnp.bfloat16), two[k])
        return carry

    lax.fori_loop(0, half, out_step, 0)

    def conv_step(r, carry):
        def add(k, total):
            value = back[k]
            return (
                total + back_one[2 * k, r] * value[:, :width]
                + back_one[2 * k + 1, r] * value[:, width:]
            )

        total = lax.fori_loop(
            0, half, add, jnp.zeros((cols, width), jnp.float32), unroll=half if half < 20 else 1
        )
        total = total.astype(jnp.bfloat16)
        for c in range(copies):
            conv[r * copies + c] = total[c * part : (c + 1) * part]
        return carry

    lax.fori_loop(0, rows, conv_step, 0)
    pl.semaphore_wait(barrier, devices - 1)

    def send_conv(d, carry):
        to = (me + d) % devices
        pltpu.make_async_remote_copy(
            src_ref=conv.at[to],
            dst_ref=conv_out.at[me],
            send_sem=sems.at[2],
            recv_sem=sems.at[3],
            device_id=peer_of(to, copies),
            device_id_type=pl.DeviceIdType.MESH,
        ).start()
        return carry

    lax.fori_loop(1, devices, send_conv, 0)
    keep = pltpu.make_async_copy(conv.at[me], conv_out.at[me], sems.at[4])
    keep.start()

    passed[...] = jnp.zeros_like(passed)

    def pass_step(r, carry):
        passed[...] += jnp.concatenate(
            [
                x[r * copies + c, 1].astype(jnp.float32) * wide[r, c * part : (c + 1) * part]
                for c in range(copies)
            ],
            axis=0,
        )
        return carry

    lax.fori_loop(0, rows, pass_step, 0)
    widen(1)

    def in_step(k, carry):
        s = spectrum(k)
        o = spec[k]
        ir, ii, outr, outi = s[:, :width], s[:, width:], o[:, :width], o[:, width:]
        cross = jnp.concatenate([outr * ir + outi * ii, outi * ir - outr * ii], axis=1)
        corr_part[k] = split_dot(over_batch(cross), two[k])
        return carry

    lax.fori_loop(0, half, in_step, 0)

    def corr_step(r, carry):
        def add(k, total):
            value = corr_part[k]
            return (
                total + corr_one[2 * k, r] * value[:, :width]
                + corr_one[2 * k + 1, r] * value[:, width:]
            )

        corr[r] = lax.fori_loop(
            0, half, add, jnp.zeros((own_ch, width), jnp.float32), unroll=half if half < 20 else 1
        )
        return carry

    lax.fori_loop(0, freq_rows, corr_step, 0)
    states = fine.shape[1] // 4
    far = lax.broadcasted_iota(jnp.int32, (freq_rows, 2 * states), 0).astype(jnp.float32) * width
    first = lax.broadcasted_iota(jnp.int32, (freq_rows, 2 * states), 1) < states
    sign = jnp.where(first, -1.0, 1.0).astype(jnp.float32)
    for c in range(own_ch):
        low = split_dot(corr[:, c, :], fine[c])
        base = low[:, : 2 * states]
        step = far * base + low[:, 2 * states :]
        for i, value in enumerate((base, step)):
            turned = pltpu.roll(value, states, 1) * sign
            total = jnp.sum(coarse[c, 0] * value + coarse[c, 1] * turned, axis=0, keepdims=True)
            pay[c : c + 1, 2 * states * i : 2 * states * (i + 1)] = total
    products = jnp.sum(over_batch(passed[...]), axis=1, keepdims=True)
    lane = lax.broadcasted_iota(jnp.int32, (own_ch, width), 1)
    pay[:, 4 * states :] = jnp.where(lane == 0, corr[0], products)

    def send_sums(d, carry):
        to = (me + d) % devices
        pltpu.make_async_remote_copy(
            src_ref=pay,
            dst_ref=sums_out.at[me],
            send_sem=sems.at[0],
            recv_sem=sems.at[1],
            device_id=peer_of(to, copies),
            device_id_type=pl.DeviceIdType.MESH,
        ).start()
        return carry

    lax.fori_loop(1, devices, send_sums, 0)
    sums_out[me] = pay[...]
    keep.wait()
    others = pl.ds(0, devices - 1)
    for sem in (2, 3):
        pltpu.make_async_copy(conv_out.at[others], conv_out.at[others], sems.at[sem]).wait()
    for sem in (0, 1):
        pltpu.make_async_copy(sums_out.at[others], sums_out.at[others], sems.at[sem]).wait()


def middle(copies, own_ch, one, back_one, corr_one, x, kern, two, fine, coarse):
    devices, _, part, width = x.shape
    rows = devices // copies
    half = rows + 1
    cols = copies * part
    lanes = fine.shape[1] + width
    vmem = pl.BlockSpec(memory_space=pltpu.VMEM)
    smem = pl.BlockSpec(memory_space=pltpu.SMEM)
    f32 = jnp.float32
    return pl.pallas_call(
        lambda *refs: middle_kernel(copies, own_ch, *refs),
        out_shape=(
            jax.ShapeDtypeStruct((devices, part, width), jnp.bfloat16),
            jax.ShapeDtypeStruct((devices, own_ch, lanes), f32),
        ),
        in_specs=[smem] * 3 + [vmem] * 5,
        out_specs=[vmem] * 2,
        scratch_shapes=[
            pltpu.VMEM((rows, cols, width), f32),
            pltpu.VMEM((half, cols, 2 * width), f32),
            pltpu.VMEM((half, cols, 2 * width), f32),
            pltpu.VMEM((devices, part, width), jnp.bfloat16),
            pltpu.VMEM((half, own_ch, 2 * width), f32),
            pltpu.VMEM((2 * rows, own_ch, width), f32),
            pltpu.VMEM((cols, width), f32),
            pltpu.VMEM((own_ch, lanes), f32),
            pltpu.SemaphoreType.DMA((5,)),
        ],
        compiler_params=pltpu.CompilerParams(
            collective_id=0, has_side_effects=True, vmem_limit_bytes=52 * 1024 * 1024
        ),
        name="middle",
    )(one, back_one, corr_one, x, kern, two, fine, coarse)


def local(inputs, out_grad, log_rate, pole_angle, weight_real, weight_imag, passthrough):
    batch_rows, slice_len, channels = inputs.shape
    rows = lax.axis_size("seq")
    copies = lax.axis_size("batch")
    devices = rows * copies
    own_ch = channels // devices
    batch = batch_rows * copies
    freq_rows = 2 * rows
    half = rows + 1
    n_freq = freq_rows * slice_len
    me = lax.axis_index("seq") * copies + lax.axis_index("batch")

    def to_parts(x):
        x = x.reshape(batch_rows, slice_len, devices, own_ch)
        return x.transpose(2, 0, 3, 1).reshape(devices, 1, batch_rows * own_ch, slice_len)

    both = jnp.concatenate([to_parts(out_grad), to_parts(inputs)], axis=1)
    both = lax.all_to_all(both, AXES, split_axis=0, concat_axis=0, tiled=True)
    k_index = jnp.arange(half, dtype=jnp.int32)
    r_index = jnp.arange(freq_rows, dtype=jnp.int32)
    m_index = jnp.arange(slice_len, dtype=jnp.int32)
    cos_one, sin_one = cos_sin(k_index[:, None] * r_index[None, :], freq_rows)
    table_one = jnp.stack([cos_one, -sin_one], axis=1)
    cos_two, sin_two = cos_sin(m_index[:, None] * m_index[None, :], slice_len)
    turn_real, turn_imag = cos_sin(k_index[:, None] * m_index[None, :], n_freq)
    full_cos = turn_real[:, :, None] * cos_two - turn_imag[:, :, None] * sin_two
    full_sin = turn_imag[:, :, None] * cos_two + turn_real[:, :, None] * sin_two
    table_two = jnp.concatenate(
        [
            jnp.concatenate([full_cos, -full_sin], axis=2),
            jnp.concatenate([full_sin, full_cos], axis=2),
        ],
        axis=1,
    )
    ends = (k_index == 0) | (k_index == rows)
    share = jnp.where(ends, 1.0, 2.0).astype(jnp.float32)[:, None, None] / n_freq
    table_back = table_one * share
    flat = (2 * half, freq_rows)
    held = table_one.astype(jnp.bfloat16).astype(jnp.float32)
    one = held.reshape(flat)
    back_one = (held * (share * n_freq)).reshape(flat)
    corr_one = table_back.reshape(flat)

    def own(p):
        return lax.dynamic_slice_in_dim(p, me * own_ch, own_ch, 0)

    all_rate = jnp.exp(log_rate)
    all_shrink = jnp.sqrt(-jnp.expm1(-2.0 * all_rate))
    rate, angle, shrink = own(all_rate), own(pole_angle), own(all_shrink)
    weight = (own(weight_real) * shrink, own(weight_imag) * shrink)
    fine = powers(rate, angle, 1.0, jnp.arange(slice_len))
    coarse = powers(rate, angle, float(slice_len), jnp.arange(freq_rows))
    whole = tuple(v[..., 0] for v in powers(rate, angle, float(slice_len), jnp.full((1,), freq_rows)))
    lam = (fine[0][..., 1], fine[1][..., 1])
    gap = (1.0 - whole[0], -whole[1])
    bottom = cmul(lam, gap)
    lead = cdiv(weight, bottom)
    tail = 2.0 * jnp.sum(cdiv(weight, lam)[0], axis=1)
    lead_rows = cmul((lead[0][..., None], lead[1][..., None]), coarse)
    taps = jnp.einsum(
        "xsr,xsm->rxm",
        jnp.concatenate([2.0 * lead_rows[0], -2.0 * lead_rows[1]], axis=1),
        jnp.concatenate(fine, axis=1),
        precision=HIGH,
    )
    kern = jnp.einsum("kir,rxm->kxim", table_one, taps, precision=HIGH)
    kern = jnp.einsum("kxa,kab->kxb", kern.reshape(half, own_ch, -1), table_two, precision=HIGH)
    shift = jnp.concatenate([jnp.ones(slice_len), jnp.zeros(slice_len)]).astype(jnp.float32)
    kern = (kern - tail[None, :, None] * shift) / n_freq
    if own_ch % 8:
        kern = jnp.tile(kern, (1, batch, 1))
    steps = jnp.arange(slice_len, dtype=jnp.float32)
    fine = jnp.concatenate([fine[0], fine[1], steps * fine[0], steps * fine[1]], axis=1)
    coarse = jnp.stack([jnp.swapaxes(v, 1, 2) for v in coarse], axis=1)
    conv, packed = middle(
        copies,
        own_ch,
        one,
        back_one,
        corr_one,
        both,
        kern,
        table_two.astype(jnp.bfloat16),
        fine.astype(jnp.bfloat16),
        jnp.concatenate([coarse, coarse], axis=3),
    )
    packed = packed.reshape(channels, -1)
    conv = conv.reshape(devices, batch_rows, own_ch, slice_len)
    conv = conv.transpose(1, 3, 0, 2).reshape(batch_rows, slice_len, channels)
    input_grad = (conv.astype(jnp.float32) + passthrough * out_grad.astype(jnp.float32)).astype(
        jnp.bfloat16
    )

    states = log_rate.shape[1]
    rate, shrink = all_rate, all_shrink
    t0 = (packed[:, :states], packed[:, states : 2 * states])
    t1 = (packed[:, 2 * states : 3 * states], packed[:, 3 * states : 4 * states])
    corr0 = packed[:, 4 * states : 4 * states + 1]
    lam = tuple(v[..., 0] for v in powers(rate, pole_angle, 1.0, jnp.full((1,), 1)))
    whole = tuple(
        v[..., 0] for v in powers(rate, pole_angle, float(slice_len), jnp.full((1,), freq_rows))
    )
    gap = (1.0 - whole[0], -whole[1])
    bottom = cmul(lam, gap)
    weight = (weight_real * shrink, weight_imag * shrink)
    near = cdiv((corr0, jnp.zeros_like(corr0)), lam)
    top = cdiv(t0, bottom)
    h = (top[0] - near[0], top[1] - near[1])
    d = cdiv(t1, bottom)
    ratio = cdiv((1.0 - (n_freq + 1.0) * whole[0], -(n_freq + 1.0) * whole[1]), gap)
    lower = cmul(top, ratio)
    d = (d[0] - lower[0] + near[0], d[1] - lower[1] + near[1])
    wd = cmul(weight, d)
    shrink_part = 2.0 * (weight_real * h[0] - weight_imag * h[1]) * jnp.exp(-2.0 * rate) / shrink
    return (
        input_grad,
        rate * (shrink_part - 2.0 * wd[0]),
        -2.0 * wd[1],
        2.0 * shrink * h[0],
        -2.0 * shrink * h[1],
        packed[:, 4 * states + 1],
    )


def solution(mesh):
    placed = (P("batch", "seq", None), P("batch", "seq", None), P(), P(), P(), P(), P())
    return jax.shard_map(
        local,
        mesh=mesh,
        in_specs=placed,
        out_specs=(P("batch", "seq", None), P(), P(), P(), P(), P()),
        check_vma=False,
    )
```

```python
import math

import jax
import jax.numpy as jnp
from jax import lax
from jax.experimental import pallas as pl
from jax.experimental.pallas import tpu as pltpu
from jax.sharding import PartitionSpec as P

TWO_PI = 2.0 * math.pi
AXES = ("seq", "batch")
HIGH = lax.Precision.HIGH


def cos_sin(numerator, length):
    phases = (numerator % length).astype(jnp.float32) * (TWO_PI / length)
    return (jnp.cos(phases), jnp.sin(phases))


def cmul(a, b):
    return (a[0] * b[0] - a[1] * b[1], a[0] * b[1] + a[1] * b[0])


def cdiv(a, b):
    inv = 1.0 / (b[0] * b[0] + b[1] * b[1])
    return ((a[0] * b[0] + a[1] * b[1]) * inv, (a[1] * b[0] - a[0] * b[1]) * inv)


def powers(rate, angle, step, counts):
    turn = angle * step
    laps = jnp.round(turn * (1.0 / TWO_PI))
    turn = (turn - laps * 6.28125) - laps * (TWO_PI - 6.28125)
    n = counts.astype(jnp.float32)
    size = jnp.exp(-(rate * step)[..., None] * n)
    phase = turn[..., None] * n
    return (size * jnp.cos(phase), size * jnp.sin(phase))


def peer_of(place, copies):
    return {"seq": place // copies, "batch": place % copies}


def nt_dot(left, right):
    return lax.dot_general(
        left, right, (((1,), (1,)), ((), ())), preferred_element_type=jnp.float32
    )


def split_dot(values, table):
    high = values.astype(jnp.bfloat16).astype(jnp.float32)
    low = values - high
    count = values.shape[0]
    if count % 8 == 0:
        both = jnp.concatenate([high, low], axis=0).astype(jnp.bfloat16)
        both = nt_dot(both, table)
        return both[:count] + both[count:]
    return nt_dot(high.astype(jnp.bfloat16), table) + nt_dot(low.astype(jnp.bfloat16), table)


def middle_kernel(
    copies, own_ch, one, back_one, corr_one, x, kern, two, fine, coarse,
    conv_out, sums_out, wide, spec, back, conv, corr_part, corr, passed, pay, sems,
):
    devices, _, part, width = x.shape
    rows = devices // copies
    half = rows + 1
    freq_rows = 2 * rows
    cols = copies * part
    me = lax.axis_index("seq") * copies + lax.axis_index("batch")
    barrier = pltpu.get_barrier_semaphore()

    def greet(d, carry):
        pl.semaphore_signal(
            barrier,
            inc=1,
            device_id=peer_of((me + d) % devices, copies),
            device_id_type=pl.DeviceIdType.MESH,
        )
        return carry

    lax.fori_loop(1, devices, greet, 0)

    def over_batch(values):
        if own_ch % 8 == 0:
            return jnp.sum(values.reshape(cols // own_ch, own_ch, -1), axis=0)
        pick = lax.broadcasted_iota(jnp.int32, (own_ch, cols), 1) % own_ch
        pick = pick == lax.broadcasted_iota(jnp.int32, (own_ch, cols), 0)
        return jnp.dot(
            pick.astype(jnp.float32), values, precision=lax.Precision.HIGHEST,
            preferred_element_type=jnp.float32,
        )

    mid = rows // 2

    def load_row(signal, r):
        return jnp.concatenate(
            [x[r * copies + c, signal].astype(jnp.float32) for c in range(copies)], axis=0
        )

    def widen(signal):
        wide[0] = load_row(signal, 0)
        wide[mid] = load_row(signal, mid)

        def one_row(r, carry):
            left, right = load_row(signal, r), load_row(signal, rows - r)
            wide[r] = left + right
            wide[mid + r] = left - right
            return carry

        lax.fori_loop(1, mid, one_row, 0)

    def spectrum(k, odd):
        def add(r, sums):
            plus, minus = wide[r], wide[mid + r]
            a, b = (minus, plus) if odd else (plus, minus)
            return (sums[0] + one[2 * k, r] * a, sums[1] + one[2 * k + 1, r] * b)

        first = one[2 * k, 0] * wide[0]
        middle_row = wide[mid]
        if odd:
            start = (first, one[2 * k + 1, mid] * middle_row)
        else:
            start = (first + one[2 * k, mid] * middle_row, jnp.zeros((cols, width), jnp.float32))
        if mid <= 16:
            g = start
            for r in range(1, mid):
                g = add(r, g)
        else:
            g = lax.fori_loop(1, mid, add, start)
        g = jnp.concatenate(g, axis=1).astype(jnp.bfloat16)
        return jnp.dot(g, two[k], preferred_element_type=jnp.float32)

    def over_freq(step):
        lax.fori_loop(0, mid + 1, lambda j, carry: step(2 * j, False, carry), 0)
        lax.fori_loop(0, mid, lambda j, carry: step(2 * j + 1, True, carry), 0)

    widen(0)

    def out_step(k, odd, carry):
        s = spectrum(k, odd)
        spec[k] = s
        kk = kern[k]
        if own_ch % 8 == 0:
            kk = jnp.broadcast_to(kk[None], (cols // own_ch,) + kk.shape).reshape(cols, 2 * width)
        sr, si, kr, ki = s[:, :width], s[:, width:], kk[:, :width], kk[:, width:]
        prod = jnp.concatenate([kr * sr + ki * si, kr * si - ki * sr], axis=1)
        back[k] = nt_dot(prod.astype(jnp.bfloat16), two[k])
        return carry

    over_freq(out_step)

    def conv_parts(r, c):
        def add(k, sums):
            value = back[k, c * part : (c + 1) * part]
            return (
                sums[0] + back_one[2 * k, r] * value[:, :width],
                sums[1] + back_one[2 * k + 1, r] * value[:, width:],
            )

        zero = jnp.zeros((part, width), jnp.float32)
        if half < 20:
            even, odd = (zero, zero), (zero, zero)
            for k in range(0, half, 2):
                even = add(k, even)
            for k in range(1, half, 2):
                odd = add(k, odd)
        else:
            even = lax.fori_loop(0, mid + 1, lambda j, v: add(2 * j, v), (zero, zero))
            odd = lax.fori_loop(0, mid, lambda j, v: add(2 * j + 1, v), (zero, zero))
        return even[0] + odd[1], odd[0] + even[1]

    def conv_step(r, carry):
        for c in range(copies):
            keep_part, flip_part = conv_parts(r, c)
            conv[r * copies + c] = (keep_part + flip_part).astype(jnp.bfloat16)
            conv[(rows - r) * copies + c] = (keep_part - flip_part).astype(jnp.bfloat16)
        return carry

    for r in (0, mid):
        for c in range(copies):
            keep_part, flip_part = conv_parts(r, c)
            conv[r * copies + c] = (keep_part + flip_part).astype(jnp.bfloat16)
    lax.fori_loop(1, mid, conv_step, 0)
    pl.semaphore_wait(barrier, devices - 1)

    def send_conv(d, carry):
        to = (me + d) % devices
        pltpu.make_async_remote_copy(
            src_ref=conv.at[to],
            dst_ref=conv_out.at[me],
            send_sem=sems.at[2],
            recv_sem=sems.at[3],
            device_id=peer_of(to, copies),
            device_id_type=pl.DeviceIdType.MESH,
        ).start()
        return carry

    lax.fori_loop(1, devices, send_conv, 0)
    keep = pltpu.make_async_copy(conv.at[me], conv_out.at[me], sems.at[4])
    keep.start()

    passed[...] = jnp.zeros_like(passed)

    def pass_step(r, carry):
        passed[...] += load_row(0, r) * load_row(1, r)
        return carry

    lax.fori_loop(0, rows, pass_step, 0)
    widen(1)

    def in_step(k, odd, carry):
        s = spectrum(k, odd)
        o = spec[k]
        ir, ii, outr, outi = s[:, :width], s[:, width:], o[:, :width], o[:, width:]
        cross = jnp.concatenate([outr * ir + outi * ii, outi * ir - outr * ii], axis=1)
        corr_part[k] = split_dot(over_batch(cross), two[k])
        return carry

    over_freq(in_step)

    def corr_step(r, carry):
        def add(k, total):
            value = corr_part[k]
            return (
                total + corr_one[2 * k, r] * value[:, :width]
                + corr_one[2 * k + 1, r] * value[:, width:]
            )

        corr[r] = lax.fori_loop(
            0, half, add, jnp.zeros((own_ch, width), jnp.float32), unroll=half if half < 20 else 1
        )
        return carry

    lax.fori_loop(0, freq_rows, corr_step, 0)
    states = fine.shape[1] // 4
    far = lax.broadcasted_iota(jnp.int32, (freq_rows, 2 * states), 0).astype(jnp.float32) * width
    first = lax.broadcasted_iota(jnp.int32, (freq_rows, 2 * states), 1) < states
    sign = jnp.where(first, -1.0, 1.0).astype(jnp.float32)
    for c in range(own_ch):
        low = split_dot(corr[:, c, :], fine[c])
        base = low[:, : 2 * states]
        step = far * base + low[:, 2 * states :]
        for i, value in enumerate((base, step)):
            turned = pltpu.roll(value, states, 1) * sign
            total = jnp.sum(coarse[c, 0] * value + coarse[c, 1] * turned, axis=0, keepdims=True)
            pay[c : c + 1, 2 * states * i : 2 * states * (i + 1)] = total
    products = jnp.sum(over_batch(passed[...]), axis=1, keepdims=True)
    lane = lax.broadcasted_iota(jnp.int32, (own_ch, width), 1)
    pay[:, 4 * states :] = jnp.where(lane == 0, corr[0], products)

    row, copy = lax.axis_index("seq"), lax.axis_index("batch")

    def send_sums(d, carry):
        pltpu.make_async_remote_copy(
            src_ref=pay,
            dst_ref=sums_out.at[copy, row],
            send_sem=sems.at[0],
            recv_sem=sems.at[1],
            device_id={"seq": (row + d) % rows, "batch": copy},
            device_id_type=pl.DeviceIdType.MESH,
        ).start()
        return carry

    lax.fori_loop(1, rows, send_sums, 0)
    sums_out[copy, row] = pay[...]
    slots = sums_out.at[0, pl.ds(0, rows - 1)]
    pltpu.make_async_copy(slots, slots, sems.at[1]).wait()

    def forward_sums(d, carry):
        pltpu.make_async_remote_copy(
            src_ref=sums_out.at[copy],
            dst_ref=sums_out.at[copy],
            send_sem=sems.at[5],
            recv_sem=sems.at[6],
            device_id={"seq": row, "batch": (copy + d) % copies},
            device_id_type=pl.DeviceIdType.MESH,
        ).start()
        return carry

    lax.fori_loop(1, copies, forward_sums, 0)
    keep.wait()
    others = pl.ds(0, devices - 1)
    for sem in (2, 3):
        pltpu.make_async_copy(conv_out.at[others], conv_out.at[others], sems.at[sem]).wait()
    pltpu.make_async_copy(slots, slots, sems.at[0]).wait()
    groups = sums_out.at[pl.ds(0, copies - 1)]
    for sem in (5, 6):
        pltpu.make_async_copy(groups, groups, sems.at[sem]).wait()


def middle(copies, own_ch, one, back_one, corr_one, x, kern, two, fine, coarse):
    devices, _, part, width = x.shape
    rows = devices // copies
    half = rows + 1
    cols = copies * part
    lanes = fine.shape[1] + width
    vmem = pl.BlockSpec(memory_space=pltpu.VMEM)
    smem = pl.BlockSpec(memory_space=pltpu.SMEM)
    f32 = jnp.float32
    return pl.pallas_call(
        lambda *refs: middle_kernel(copies, own_ch, *refs),
        out_shape=(
            jax.ShapeDtypeStruct((devices, part, width), jnp.bfloat16),
            jax.ShapeDtypeStruct((copies, rows, own_ch, lanes), f32),
        ),
        in_specs=[smem] * 3 + [vmem] * 5,
        out_specs=[vmem] * 2,
        scratch_shapes=[
            pltpu.VMEM((rows, cols, width), f32),
            pltpu.VMEM((half, cols, 2 * width), f32),
            pltpu.VMEM((half, cols, 2 * width), f32),
            pltpu.VMEM((devices, part, width), jnp.bfloat16),
            pltpu.VMEM((half, own_ch, 2 * width), f32),
            pltpu.VMEM((2 * rows, own_ch, width), f32),
            pltpu.VMEM((cols, width), f32),
            pltpu.VMEM((own_ch, lanes), f32),
            pltpu.SemaphoreType.DMA((7,)),
        ],
        compiler_params=pltpu.CompilerParams(
            collective_id=0, has_side_effects=True, vmem_limit_bytes=52 * 1024 * 1024
        ),
        name="middle",
    )(one, back_one, corr_one, x, kern, two, fine, coarse)


def local(inputs, out_grad, log_rate, pole_angle, weight_real, weight_imag, passthrough):
    batch_rows, slice_len, channels = inputs.shape
    rows = lax.axis_size("seq")
    copies = lax.axis_size("batch")
    devices = rows * copies
    own_ch = channels // devices
    batch = batch_rows * copies
    freq_rows = 2 * rows
    half = rows + 1
    n_freq = freq_rows * slice_len
    me = lax.axis_index("seq") * copies + lax.axis_index("batch")

    def to_parts(x):
        x = x.reshape(batch_rows, slice_len, devices, own_ch)
        return x.transpose(2, 0, 3, 1).reshape(devices, 1, batch_rows * own_ch, slice_len)

    both = jnp.concatenate([to_parts(out_grad), to_parts(inputs)], axis=1)
    both = lax.all_to_all(both, AXES, split_axis=0, concat_axis=0, tiled=True)
    k_index = jnp.arange(half, dtype=jnp.int32)
    r_index = jnp.arange(freq_rows, dtype=jnp.int32)
    m_index = jnp.arange(slice_len, dtype=jnp.int32)
    cos_one, sin_one = cos_sin(k_index[:, None] * r_index[None, :], freq_rows)
    table_one = jnp.stack([cos_one, -sin_one], axis=1)
    cos_two, sin_two = cos_sin(m_index[:, None] * m_index[None, :], slice_len)
    turn_real, turn_imag = cos_sin(k_index[:, None] * m_index[None, :], n_freq)
    full_cos = turn_real[:, :, None] * cos_two - turn_imag[:, :, None] * sin_two
    full_sin = turn_imag[:, :, None] * cos_two + turn_real[:, :, None] * sin_two
    table_two = jnp.concatenate(
        [
            jnp.concatenate([full_cos, -full_sin], axis=2),
            jnp.concatenate([full_sin, full_cos], axis=2),
        ],
        axis=1,
    )
    ends = (k_index == 0) | (k_index == rows)
    share = jnp.where(ends, 1.0, 2.0).astype(jnp.float32)[:, None, None] / n_freq
    table_back = table_one * share
    flat = (2 * half, freq_rows)
    held = table_one.astype(jnp.bfloat16).astype(jnp.float32)
    one = held.reshape(flat)
    back_one = (held * (share * n_freq)).reshape(flat)
    corr_one = table_back.reshape(flat)

    def own(p):
        return lax.dynamic_slice_in_dim(p, me * own_ch, own_ch, 0)

    all_rate = jnp.exp(log_rate)
    all_shrink = jnp.sqrt(-jnp.expm1(-2.0 * all_rate))
    rate, angle, shrink = own(all_rate), own(pole_angle), own(all_shrink)
    weight = (own(weight_real) * shrink, own(weight_imag) * shrink)
    fine = powers(rate, angle, 1.0, jnp.arange(slice_len))
    coarse = powers(rate, angle, float(slice_len), jnp.arange(freq_rows))
    whole = tuple(v[..., 0] for v in powers(rate, angle, float(slice_len), jnp.full((1,), freq_rows)))
    lam = (fine[0][..., 1], fine[1][..., 1])
    gap = (1.0 - whole[0], -whole[1])
    bottom = cmul(lam, gap)
    lead = cdiv(weight, bottom)
    tail = 2.0 * jnp.sum(cdiv(weight, lam)[0], axis=1)
    lead_rows = cmul((lead[0][..., None], lead[1][..., None]), coarse)
    taps = jnp.einsum(
        "xsr,xsm->rxm",
        jnp.concatenate([2.0 * lead_rows[0], -2.0 * lead_rows[1]], axis=1),
        jnp.concatenate(fine, axis=1),
        precision=HIGH,
    )
    kern = jnp.einsum("kir,rxm->kxim", table_one, taps, precision=HIGH)
    kern = jnp.einsum("kxa,kab->kxb", kern.reshape(half, own_ch, -1), table_two, precision=HIGH)
    shift = jnp.concatenate([jnp.ones(slice_len), jnp.zeros(slice_len)]).astype(jnp.float32)
    kern = (kern - tail[None, :, None] * shift) / n_freq
    if own_ch % 8:
        kern = jnp.tile(kern, (1, batch, 1))
    steps = jnp.arange(slice_len, dtype=jnp.float32)
    fine = jnp.concatenate([fine[0], fine[1], steps * fine[0], steps * fine[1]], axis=1)
    coarse = jnp.stack([jnp.swapaxes(v, 1, 2) for v in coarse], axis=1)
    conv, packed = middle(
        copies,
        own_ch,
        one,
        back_one,
        corr_one,
        both,
        kern,
        table_two.astype(jnp.bfloat16),
        fine.astype(jnp.bfloat16),
        jnp.concatenate([coarse, coarse], axis=3),
    )
    packed = jnp.swapaxes(packed, 0, 1).reshape(channels, -1)
    conv = conv.reshape(devices, batch_rows, own_ch, slice_len)
    conv = conv.transpose(1, 3, 0, 2).reshape(batch_rows, slice_len, channels)
    input_grad = (conv.astype(jnp.float32) + passthrough * out_grad.astype(jnp.float32)).astype(
        jnp.bfloat16
    )

    states = log_rate.shape[1]
    rate, shrink = all_rate, all_shrink
    t0 = (packed[:, :states], packed[:, states : 2 * states])
    t1 = (packed[:, 2 * states : 3 * states], packed[:, 3 * states : 4 * states])
    corr0 = packed[:, 4 * states : 4 * states + 1]
    lam = tuple(v[..., 0] for v in powers(rate, pole_angle, 1.0, jnp.full((1,), 1)))
    whole = tuple(
        v[..., 0] for v in powers(rate, pole_angle, float(slice_len), jnp.full((1,), freq_rows))
    )
    gap = (1.0 - whole[0], -whole[1])
    bottom = cmul(lam, gap)
    weight = (weight_real * shrink, weight_imag * shrink)
    near = cdiv((corr0, jnp.zeros_like(corr0)), lam)
    top = cdiv(t0, bottom)
    h = (top[0] - near[0], top[1] - near[1])
    d = cdiv(t1, bottom)
    ratio = cdiv((1.0 - (n_freq + 1.0) * whole[0], -(n_freq + 1.0) * whole[1]), gap)
    lower = cmul(top, ratio)
    d = (d[0] - lower[0] + near[0], d[1] - lower[1] + near[1])
    wd = cmul(weight, d)
    shrink_part = 2.0 * (weight_real * h[0] - weight_imag * h[1]) * jnp.exp(-2.0 * rate) / shrink
    return (
        input_grad,
        rate * (shrink_part - 2.0 * wd[0]),
        -2.0 * wd[1],
        2.0 * shrink * h[0],
        -2.0 * shrink * h[1],
        packed[:, 4 * states + 1],
    )


def solution(mesh):
    placed = (P("batch", "seq", None), P("batch", "seq", None), P(), P(), P(), P(), P())
    return jax.shard_map(
        local,
        mesh=mesh,
        in_specs=placed,
        out_specs=(P("batch", "seq", None), P(), P(), P(), P(), P()),
        check_vma=False,
    )
```

```python
import math

import jax
import jax.numpy as jnp
from jax import lax
from jax.experimental import pallas as pl
from jax.experimental.pallas import tpu as pltpu
from jax.sharding import PartitionSpec as P

TWO_PI = 2.0 * math.pi
AXES = ("seq", "batch")
HIGH = lax.Precision.HIGH


def cos_sin(numerator, length):
    phases = (numerator % length).astype(jnp.float32) * (TWO_PI / length)
    return (jnp.cos(phases), jnp.sin(phases))


def cmul(a, b):
    return (a[0] * b[0] - a[1] * b[1], a[0] * b[1] + a[1] * b[0])


def cdiv(a, b):
    inv = 1.0 / (b[0] * b[0] + b[1] * b[1])
    return ((a[0] * b[0] + a[1] * b[1]) * inv, (a[1] * b[0] - a[0] * b[1]) * inv)


def powers(rate, angle, step, counts):
    turn = angle * step
    laps = jnp.round(turn * (1.0 / TWO_PI))
    turn = (turn - laps * 6.28125) - laps * (TWO_PI - 6.28125)
    n = counts.astype(jnp.float32)
    size = jnp.exp(-(rate * step)[..., None] * n)
    phase = turn[..., None] * n
    return (size * jnp.cos(phase), size * jnp.sin(phase))


def peer_of(place, copies):
    return {"seq": place // copies, "batch": place % copies}


def nt_dot(left, right):
    return lax.dot_general(
        left, right, (((1,), (1,)), ((), ())), preferred_element_type=jnp.float32
    )


def split_dot(values, table):
    high = values.astype(jnp.bfloat16).astype(jnp.float32)
    low = values - high
    count = values.shape[0]
    if count % 8 == 0:
        both = jnp.concatenate([high, low], axis=0).astype(jnp.bfloat16)
        both = nt_dot(both, table)
        return both[:count] + both[count:]
    return nt_dot(high.astype(jnp.bfloat16), table) + nt_dot(low.astype(jnp.bfloat16), table)


def middle_kernel(
    copies, own_ch, one, back_one, corr_one, x, kern, two, fine, coarse,
    conv_out, sums_out, wide, spec, back, conv, corr_part, corr, passed, pay, sems,
):
    devices, _, part, width = x.shape
    rows = devices // copies
    half = rows + 1
    freq_rows = 2 * rows
    cols = copies * part
    me = lax.axis_index("seq") * copies + lax.axis_index("batch")
    barrier = pltpu.get_barrier_semaphore()

    def greet(d, carry):
        pl.semaphore_signal(
            barrier,
            inc=1,
            device_id=peer_of((me + d) % devices, copies),
            device_id_type=pl.DeviceIdType.MESH,
        )
        return carry

    lax.fori_loop(1, devices, greet, 0)

    def over_batch(values):
        if own_ch % 8 == 0:
            return jnp.sum(values.reshape(cols // own_ch, own_ch, -1), axis=0)
        pick = lax.broadcasted_iota(jnp.int32, (own_ch, cols), 1) % own_ch
        pick = pick == lax.broadcasted_iota(jnp.int32, (own_ch, cols), 0)
        return jnp.dot(
            pick.astype(jnp.float32), values, precision=lax.Precision.HIGHEST,
            preferred_element_type=jnp.float32,
        )

    mid = rows // 2

    def load_row(signal, r):
        return jnp.concatenate(
            [x[r * copies + c, signal].astype(jnp.float32) for c in range(copies)], axis=0
        )

    def widen(signal):
        wide[0] = load_row(signal, 0)
        wide[mid] = load_row(signal, mid)

        def one_row(r, carry):
            left, right = load_row(signal, r), load_row(signal, rows - r)
            wide[r] = left + right
            wide[mid + r] = left - right
            return carry

        lax.fori_loop(1, mid, one_row, 0)

    def spectrum(k, odd):
        def add(r, sums):
            plus, minus = wide[r], wide[mid + r]
            a, b = (minus, plus) if odd else (plus, minus)
            return (sums[0] + one[2 * k, r] * a, sums[1] + one[2 * k + 1, r] * b)

        first = one[2 * k, 0] * wide[0]
        middle_row = wide[mid]
        if odd:
            start = (first, one[2 * k + 1, mid] * middle_row)
        else:
            start = (first + one[2 * k, mid] * middle_row, jnp.zeros((cols, width), jnp.float32))
        if mid <= 16:
            g = start
            for r in range(1, mid):
                g = add(r, g)
        else:
            g = lax.fori_loop(1, mid, add, start)
        g = jnp.concatenate(g, axis=1).astype(jnp.bfloat16)
        return jnp.dot(g, two[k], preferred_element_type=jnp.float32)

    def over_freq(step):
        for odd, count in ((False, mid + 1), (True, mid)):
            group = next(u for u in (3, 2, 1) if count % u == 0)

            def several(j, carry, odd=odd, group=group):
                for u in range(group):
                    carry = step(2 * (group * j + u) + int(odd), odd, carry)
                return carry

            lax.fori_loop(0, count // group, several, 0)

    widen(0)

    def out_step(k, odd, carry):
        s = spectrum(k, odd)
        spec[k] = s
        kk = kern[k]
        if own_ch % 8 == 0:
            kk = jnp.broadcast_to(kk[None], (cols // own_ch,) + kk.shape).reshape(cols, 2 * width)
        sr, si, kr, ki = s[:, :width], s[:, width:], kk[:, :width], kk[:, width:]
        prod = jnp.concatenate([kr * sr + ki * si, kr * si - ki * sr], axis=1)
        back[k] = nt_dot(prod.astype(jnp.bfloat16), two[k])
        return carry

    over_freq(out_step)

    def conv_parts(r, c):
        def add(k, sums):
            value = back[k, c * part : (c + 1) * part]
            return (
                sums[0] + back_one[2 * k, r] * value[:, :width],
                sums[1] + back_one[2 * k + 1, r] * value[:, width:],
            )

        zero = jnp.zeros((part, width), jnp.float32)
        if half < 20:
            even, odd = (zero, zero), (zero, zero)
            for k in range(0, half, 2):
                even = add(k, even)
            for k in range(1, half, 2):
                odd = add(k, odd)
        else:
            even = lax.fori_loop(0, mid + 1, lambda j, v: add(2 * j, v), (zero, zero))
            odd = lax.fori_loop(0, mid, lambda j, v: add(2 * j + 1, v), (zero, zero))
        return even[0] + odd[1], odd[0] + even[1]

    def conv_step(r, carry):
        for c in range(copies):
            keep_part, flip_part = conv_parts(r, c)
            conv[r * copies + c] = (keep_part + flip_part).astype(jnp.bfloat16)
            conv[(rows - r) * copies + c] = (keep_part - flip_part).astype(jnp.bfloat16)
        return carry

    for r in (0, mid):
        for c in range(copies):
            keep_part, flip_part = conv_parts(r, c)
            conv[r * copies + c] = (keep_part + flip_part).astype(jnp.bfloat16)
    lax.fori_loop(1, mid, conv_step, 0)
    pl.semaphore_wait(barrier, devices - 1)

    def send_conv(d, carry):
        to = (me + d) % devices
        pltpu.make_async_remote_copy(
            src_ref=conv.at[to],
            dst_ref=conv_out.at[me],
            send_sem=sems.at[2],
            recv_sem=sems.at[3],
            device_id=peer_of(to, copies),
            device_id_type=pl.DeviceIdType.MESH,
        ).start()
        return carry

    lax.fori_loop(1, devices, send_conv, 0)
    keep = pltpu.make_async_copy(conv.at[me], conv_out.at[me], sems.at[4])
    keep.start()

    passed[...] = jnp.zeros_like(passed)

    def pass_step(r, carry):
        passed[...] += load_row(0, r) * load_row(1, r)
        return carry

    lax.fori_loop(0, rows, pass_step, 0)
    widen(1)

    def in_step(k, odd, carry):
        s = spectrum(k, odd)
        o = spec[k]
        ir, ii, outr, outi = s[:, :width], s[:, width:], o[:, :width], o[:, width:]
        cross = jnp.concatenate([outr * ir + outi * ii, outi * ir - outr * ii], axis=1)
        corr_part[k] = split_dot(over_batch(cross), two[k])
        return carry

    over_freq(in_step)

    def corr_step(r, carry):
        def add(k, total):
            value = corr_part[k]
            return (
                total + corr_one[2 * k, r] * value[:, :width]
                + corr_one[2 * k + 1, r] * value[:, width:]
            )

        corr[r] = lax.fori_loop(
            0, half, add, jnp.zeros((own_ch, width), jnp.float32), unroll=half if half < 20 else 1
        )
        return carry

    lax.fori_loop(0, freq_rows, corr_step, 0)
    states = fine.shape[1] // 4
    far = lax.broadcasted_iota(jnp.int32, (freq_rows, 2 * states), 0).astype(jnp.float32) * width
    first = lax.broadcasted_iota(jnp.int32, (freq_rows, 2 * states), 1) < states
    sign = jnp.where(first, -1.0, 1.0).astype(jnp.float32)
    for c in range(own_ch):
        low = split_dot(corr[:, c, :], fine[c])
        base = low[:, : 2 * states]
        step = far * base + low[:, 2 * states :]
        for i, value in enumerate((base, step)):
            turned = pltpu.roll(value, states, 1) * sign
            total = jnp.sum(coarse[c, 0] * value + coarse[c, 1] * turned, axis=0, keepdims=True)
            pay[c : c + 1, 2 * states * i : 2 * states * (i + 1)] = total
    products = jnp.sum(over_batch(passed[...]), axis=1, keepdims=True)
    lane = lax.broadcasted_iota(jnp.int32, (own_ch, width), 1)
    pay[:, 4 * states :] = jnp.where(lane == 0, corr[0], products)

    row, copy = lax.axis_index("seq"), lax.axis_index("batch")

    def send_sums(d, carry):
        pltpu.make_async_remote_copy(
            src_ref=pay,
            dst_ref=sums_out.at[copy, row],
            send_sem=sems.at[0],
            recv_sem=sems.at[1],
            device_id={"seq": (row + d) % rows, "batch": copy},
            device_id_type=pl.DeviceIdType.MESH,
        ).start()
        return carry

    lax.fori_loop(1, rows, send_sums, 0)
    sums_out[copy, row] = pay[...]
    slots = sums_out.at[0, pl.ds(0, rows - 1)]
    pltpu.make_async_copy(slots, slots, sems.at[1]).wait()

    def forward_sums(d, carry):
        pltpu.make_async_remote_copy(
            src_ref=sums_out.at[copy],
            dst_ref=sums_out.at[copy],
            send_sem=sems.at[5],
            recv_sem=sems.at[6],
            device_id={"seq": row, "batch": (copy + d) % copies},
            device_id_type=pl.DeviceIdType.MESH,
        ).start()
        return carry

    lax.fori_loop(1, copies, forward_sums, 0)
    keep.wait()
    others = pl.ds(0, devices - 1)
    for sem in (2, 3):
        pltpu.make_async_copy(conv_out.at[others], conv_out.at[others], sems.at[sem]).wait()
    pltpu.make_async_copy(slots, slots, sems.at[0]).wait()
    groups = sums_out.at[pl.ds(0, copies - 1)]
    for sem in (5, 6):
        pltpu.make_async_copy(groups, groups, sems.at[sem]).wait()


def middle(copies, own_ch, one, back_one, corr_one, x, kern, two, fine, coarse):
    devices, _, part, width = x.shape
    rows = devices // copies
    half = rows + 1
    cols = copies * part
    lanes = fine.shape[1] + width
    vmem = pl.BlockSpec(memory_space=pltpu.VMEM)
    smem = pl.BlockSpec(memory_space=pltpu.SMEM)
    f32 = jnp.float32
    return pl.pallas_call(
        lambda *refs: middle_kernel(copies, own_ch, *refs),
        out_shape=(
            jax.ShapeDtypeStruct((devices, part, width), jnp.bfloat16),
            jax.ShapeDtypeStruct((copies, rows, own_ch, lanes), f32),
        ),
        in_specs=[smem] * 3 + [vmem] * 5,
        out_specs=[vmem] * 2,
        scratch_shapes=[
            pltpu.VMEM((rows, cols, width), f32),
            pltpu.VMEM((half, cols, 2 * width), f32),
            pltpu.VMEM((half, cols, 2 * width), f32),
            pltpu.VMEM((devices, part, width), jnp.bfloat16),
            pltpu.VMEM((half, own_ch, 2 * width), f32),
            pltpu.VMEM((2 * rows, own_ch, width), f32),
            pltpu.VMEM((cols, width), f32),
            pltpu.VMEM((own_ch, lanes), f32),
            pltpu.SemaphoreType.DMA((7,)),
        ],
        compiler_params=pltpu.CompilerParams(
            collective_id=0, has_side_effects=True, vmem_limit_bytes=52 * 1024 * 1024
        ),
        name="middle",
    )(one, back_one, corr_one, x, kern, two, fine, coarse)


def local(inputs, out_grad, log_rate, pole_angle, weight_real, weight_imag, passthrough):
    batch_rows, slice_len, channels = inputs.shape
    rows = lax.axis_size("seq")
    copies = lax.axis_size("batch")
    devices = rows * copies
    own_ch = channels // devices
    batch = batch_rows * copies
    freq_rows = 2 * rows
    half = rows + 1
    n_freq = freq_rows * slice_len
    me = lax.axis_index("seq") * copies + lax.axis_index("batch")

    def to_parts(x):
        x = x.reshape(batch_rows, slice_len, devices, own_ch)
        return x.transpose(2, 0, 3, 1).reshape(devices, 1, batch_rows * own_ch, slice_len)

    both = jnp.concatenate([to_parts(out_grad), to_parts(inputs)], axis=1)
    both = lax.all_to_all(both, AXES, split_axis=0, concat_axis=0, tiled=True)
    k_index = jnp.arange(half, dtype=jnp.int32)
    r_index = jnp.arange(freq_rows, dtype=jnp.int32)
    m_index = jnp.arange(slice_len, dtype=jnp.int32)
    cos_one, sin_one = cos_sin(k_index[:, None] * r_index[None, :], freq_rows)
    table_one = jnp.stack([cos_one, -sin_one], axis=1)
    cos_two, sin_two = cos_sin(m_index[:, None] * m_index[None, :], slice_len)
    turn_real, turn_imag = cos_sin(k_index[:, None] * m_index[None, :], n_freq)
    full_cos = turn_real[:, :, None] * cos_two - turn_imag[:, :, None] * sin_two
    full_sin = turn_imag[:, :, None] * cos_two + turn_real[:, :, None] * sin_two
    table_two = jnp.concatenate(
        [
            jnp.concatenate([full_cos, -full_sin], axis=2),
            jnp.concatenate([full_sin, full_cos], axis=2),
        ],
        axis=1,
    )
    ends = (k_index == 0) | (k_index == rows)
    share = jnp.where(ends, 1.0, 2.0).astype(jnp.float32)[:, None, None] / n_freq
    table_back = table_one * share
    flat = (2 * half, freq_rows)
    held = table_one.astype(jnp.bfloat16).astype(jnp.float32)
    one = held.reshape(flat)
    back_one = (held * (share * n_freq)).reshape(flat)
    corr_one = table_back.reshape(flat)

    def own(p):
        return lax.dynamic_slice_in_dim(p, me * own_ch, own_ch, 0)

    all_rate = jnp.exp(log_rate)
    all_shrink = jnp.sqrt(-jnp.expm1(-2.0 * all_rate))
    rate, angle, shrink = own(all_rate), own(pole_angle), own(all_shrink)
    weight = (own(weight_real) * shrink, own(weight_imag) * shrink)
    fine = powers(rate, angle, 1.0, jnp.arange(slice_len))
    coarse = powers(rate, angle, float(slice_len), jnp.arange(freq_rows))
    whole = tuple(v[..., 0] for v in powers(rate, angle, float(slice_len), jnp.full((1,), freq_rows)))
    lam = (fine[0][..., 1], fine[1][..., 1])
    gap = (1.0 - whole[0], -whole[1])
    bottom = cmul(lam, gap)
    lead = cdiv(weight, bottom)
    tail = 2.0 * jnp.sum(cdiv(weight, lam)[0], axis=1)
    lead_rows = cmul((lead[0][..., None], lead[1][..., None]), coarse)
    taps = jnp.einsum(
        "xsr,xsm->rxm",
        jnp.concatenate([2.0 * lead_rows[0], -2.0 * lead_rows[1]], axis=1),
        jnp.concatenate(fine, axis=1),
        precision=HIGH,
    )
    kern = jnp.einsum("kir,rxm->kxim", table_one, taps, precision=HIGH)
    kern = jnp.einsum("kxa,kab->kxb", kern.reshape(half, own_ch, -1), table_two, precision=HIGH)
    shift = jnp.concatenate([jnp.ones(slice_len), jnp.zeros(slice_len)]).astype(jnp.float32)
    kern = (kern - tail[None, :, None] * shift) / n_freq
    if own_ch % 8:
        kern = jnp.tile(kern, (1, batch, 1))
    steps = jnp.arange(slice_len, dtype=jnp.float32)
    fine = jnp.concatenate([fine[0], fine[1], steps * fine[0], steps * fine[1]], axis=1)
    coarse = jnp.stack([jnp.swapaxes(v, 1, 2) for v in coarse], axis=1)
    conv, packed = middle(
        copies,
        own_ch,
        one,
        back_one,
        corr_one,
        both,
        kern,
        table_two.astype(jnp.bfloat16),
        fine.astype(jnp.bfloat16),
        jnp.concatenate([coarse, coarse], axis=3),
    )
    packed = jnp.swapaxes(packed, 0, 1).reshape(channels, -1)
    conv = conv.reshape(devices, batch_rows, own_ch, slice_len)
    conv = conv.transpose(1, 3, 0, 2).reshape(batch_rows, slice_len, channels)
    input_grad = (conv.astype(jnp.float32) + passthrough * out_grad.astype(jnp.float32)).astype(
        jnp.bfloat16
    )

    states = log_rate.shape[1]
    rate, shrink = all_rate, all_shrink
    t0 = (packed[:, :states], packed[:, states : 2 * states])
    t1 = (packed[:, 2 * states : 3 * states], packed[:, 3 * states : 4 * states])
    corr0 = packed[:, 4 * states : 4 * states + 1]
    lam = tuple(v[..., 0] for v in powers(rate, pole_angle, 1.0, jnp.full((1,), 1)))
    whole = tuple(
        v[..., 0] for v in powers(rate, pole_angle, float(slice_len), jnp.full((1,), freq_rows))
    )
    gap = (1.0 - whole[0], -whole[1])
    bottom = cmul(lam, gap)
    weight = (weight_real * shrink, weight_imag * shrink)
    near = cdiv((corr0, jnp.zeros_like(corr0)), lam)
    top = cdiv(t0, bottom)
    h = (top[0] - near[0], top[1] - near[1])
    d = cdiv(t1, bottom)
    ratio = cdiv((1.0 - (n_freq + 1.0) * whole[0], -(n_freq + 1.0) * whole[1]), gap)
    lower = cmul(top, ratio)
    d = (d[0] - lower[0] + near[0], d[1] - lower[1] + near[1])
    wd = cmul(weight, d)
    shrink_part = 2.0 * (weight_real * h[0] - weight_imag * h[1]) * jnp.exp(-2.0 * rate) / shrink
    return (
        input_grad,
        rate * (shrink_part - 2.0 * wd[0]),
        -2.0 * wd[1],
        2.0 * shrink * h[0],
        -2.0 * shrink * h[1],
        packed[:, 4 * states + 1],
    )


def solution(mesh):
    placed = (P("batch", "seq", None), P("batch", "seq", None), P(), P(), P(), P(), P())
    return jax.shard_map(
        local,
        mesh=mesh,
        in_specs=placed,
        out_specs=(P("batch", "seq", None), P(), P(), P(), P(), P()),
        check_vma=False,
    )
```
